128 devices in a mesh: rep: 16 (over y_hi, x, core), fsdp: 8 (over y_lo, z).
Axes of the slice: x: 4, y: 4 (y_hi: 2, y_lo: 2; y = y_hi * 2 + y_lo), z: 4, core: 2. Of those that a mesh axis runs over, the one named last changes fastest.
Arguments:
- tokens: bfloat16 [65536, 6144], P(('rep', 'fsdp')), may hold values from -6 to 6
- norm_gain: float32 [6144], replicated, may hold values from 0.1 to 1.9
- key_weight: bfloat16 [16, 6144, 1024], P('rep', 'fsdp'), may hold values from -0.078125 to 0.078125
- key_gain: float32 [128], replicated, may hold values from 0.1 to 1.9
- key_cotangent: bfloat16 [65536, 1024], P(('rep', 'fsdp')), may hold values from -0.09375 to 0.09375
- local_fragment: bfloat16 [16, 6144, 3072], P('rep', 'fsdp'), may hold values from -6 to 6
- synced_fragment: bfloat16 [6144, 3072], P('fsdp'), may hold values from -6 to 6
- outer_momentum: float32 [6144, 3072], P(('fsdp', 'rep')), may hold values from -3 to 3
Outputs:
- key_gradient: bfloat16 [16, 6144, 1024], P('rep', 'fsdp')
- new_synced: bfloat16 [6144, 3072], P('fsdp')
- new_momentum: float32 [6144, 3072], P(('fsdp', 'rep'))
The draws below stay inside these ranges and needn't reach their ends.
All inputs are finite; a program needn't handle non-finite values. Where the reference program divides by a largest or mean magnitude, that divisor is 1e-20 or more.
Results may differ from the reference program's by a relative error of at most 0.012.
Values may be sent and summed in bfloat16 or wider, within the bound.
No kernel may reach another device: no remote copies, remote signals or barrier semaphores. Data moves between devices by JAX's collectives and lax.ppermute only.
A program may use at most 192 MiB of HBM per device.

```python
import jax
import jax.numpy as jnp
from jax import lax

D = 6144
HEAD = 128
C = 3072
BLOCK = 128
TOK_DEV = 512
KW = 1024
TOKENS = 65536
N_REP = 16
N_FSDP = 8


def block_levels(stream_key, dims, split, least, top_value):
    def one(position, blocks):
        heights = jax.random.uniform(jax.random.fold_in(jax.random.fold_in(stream_key, 6), position), (blocks,), jnp.float32, least / len(split), top_value / len(split))
        return jnp.repeat(jnp.exp(heights), dims[position] // blocks).reshape((-1,) + (1,) * (len(dims) - position - 1))

    loudness = one(*split[0])
    for cut in split[1:]:
        loudness = loudness * one(*cut)
    return loudness


def noise(stream_key, shape, width, most, cuts=(), dtype=jnp.bfloat16):
    values = width * jax.random.normal(stream_key, shape, jnp.float32)
    if cuts:
        values = values * block_levels(stream_key, shape, cuts, -0.22, 0.18)
    return jnp.clip(values, -most, most).astype(dtype)


def setup_inputs(seed: int = 0) -> dict:
    splits = jax.random.split(jax.random.key(seed), 9)
    return {
        "tokens": noise(splits[0], (TOKENS, D), 1.0, 6.0, ((0, 128),)),
        "norm_gain": jnp.clip(1.0 + 0.18 * jax.random.normal(splits[1], (D,), jnp.float32), 0.1, 1.9),
        "key_weight": noise(splits[2], (N_REP, D, KW), D ** -0.5, 0.078125, ((0, 16), (1, 8))),
        "key_gain": jnp.clip(1.0 + 0.18 * jax.random.normal(splits[3], (HEAD,), jnp.float32), 0.1, 1.9),
        "key_cotangent": noise(splits[4], (TOKENS, KW), (1.0 / (TOK_DEV * N_FSDP) ** 0.5), 0.09375, ((0, 128),)),
        "local_fragment": noise(splits[5], (N_REP, D, C), 1.0, 6.0, ((0, 16), (1, 8))),
        "synced_fragment": noise(splits[6], (D, C), 1.0, 6.0, ((0, 8),)),
        "outer_momentum": noise(splits[7], (D, C), 0.5, 3.0, ((0, 128),), jnp.float32),
    }


NORM_EPSILON = 1e-05
SCALE_EPSILON = 1e-06
OUTER_RATE = 0.7
MOMENTUM_DECAY = 0.9

def rms_rows(values, gain):
    floats = values.astype(jnp.float32)
    mean_sq = lax.optimization_barrier(jnp.mean(floats * floats, axis=-1, keepdims=True))
    return floats * lax.rsqrt(mean_sq + NORM_EPSILON) * gain.astype(jnp.float32)

def head_norm(keys, key_gain):
    shaped = keys.reshape(keys.shape[0], -1, key_gain.shape[0])
    mean_sq = lax.optimization_barrier(jnp.mean(shaped * shaped, axis=-1, keepdims=True))
    return (shaped * lax.rsqrt(mean_sq + NORM_EPSILON) * key_gain).reshape(keys.shape)

def block_terms(deltas):
    blocks = deltas.reshape(deltas.shape[0], -1, BLOCK)
    scales = (lax.optimization_barrier(jnp.max(jnp.abs(blocks), axis=-1)) + SCALE_EPSILON).astype(jnp.bfloat16)
    scales = lax.optimization_barrier(scales)
    levels = (blocks / scales.astype(jnp.float32)[..., None]).astype(jnp.bfloat16)
    levels = lax.optimization_barrier(levels)
    terms = levels.astype(jnp.float32) * scales.astype(jnp.float32)[..., None]
    return terms.reshape(deltas.shape)

def reference(tokens, norm_gain, key_weight, key_gain, key_cotangent, local_fragment, synced_fragment, outer_momentum):
    token_groups = tokens.reshape(N_REP, N_FSDP * TOK_DEV, D)
    back_groups = key_cotangent.reshape(N_REP, N_FSDP * TOK_DEV, KW)

    def one_replica(inputs):
        rows_in, weight, cotangent = inputs
        normed = rms_rows(rows_in, norm_gain).astype(jnp.bfloat16)
        keys = jnp.dot(normed, weight, preferred_element_type=jnp.float32)
        _, pull_back = jax.vjp(lambda value: head_norm(value, key_gain), keys)
        key_back, = pull_back(cotangent.astype(jnp.float32))
        key_back = key_back.astype(jnp.bfloat16)
        total = jnp.dot(normed.T, key_back, preferred_element_type=jnp.float32)
        return total.astype(jnp.bfloat16)
    key_gradient = lax.map(one_replica, (token_groups, key_weight, back_groups))
    synced = synced_fragment.astype(jnp.float32)

    def add_replica(summed, local):
        deltas = synced - local.astype(jnp.float32)
        return (summed + block_terms(deltas), None)
    summed, _ = lax.scan(add_replica, jnp.zeros((D, C), jnp.float32), local_fragment)
    mean_delta = summed / N_REP
    new_momentum = MOMENTUM_DECAY * outer_momentum + mean_delta
    new_synced = (synced - OUTER_RATE * (mean_delta + MOMENTUM_DECAY * new_momentum)).astype(jnp.bfloat16)
    return (key_gradient, new_synced, new_momentum)
```

```python
import functools

import jax
import jax.numpy as jnp
from jax import lax
from jax.experimental import pallas as pl
from jax.experimental.pallas import tpu as pltpu
from jax.sharding import Mesh, PartitionSpec as P

BLOCK = 128
HEAD = 128

NORM_EPSILON = 1e-05
SCALE_EPSILON = 1e-06
OUTER_RATE = 0.7
MOMENTUM_DECAY = 0.9

AXES = ("yh", "x", "c", "yl", "z")
REP = ("yh", "x", "c")
FSDP = ("yl", "z")
CHUNKS = (256, 256, 256, 256)

F32 = jnp.float32
BF16 = jnp.bfloat16


def shift(value, axis, size, step):
    return lax.ppermute(value, axis, [(i, (i + step) % size) for i in range(size)])


def up(value, axis):
    return shift(value, axis, 4, 1)


def down(value, axis):
    return shift(value, axis, 4, 3)


def swap(value, axis):
    return shift(value, axis, 2, 1)


def block_terms(synced, local):
    delta = synced.astype(F32) - local.astype(F32)
    top = jnp.max(jnp.abs(delta), axis=-1, keepdims=True)
    scale = (top + SCALE_EPSILON).astype(BF16).astype(F32)
    level = (delta / scale).astype(BF16).astype(F32)
    return level * scale


def terms_kernel(half_ref, synced_ref, local_ref, out_ref):
    for start in range(0, out_ref.shape[-1], BLOCK):
        at = (0, slice(None), slice(start, start + BLOCK))
        src = (0, 0, slice(None), slice(start, start + BLOCK))
        out_ref[at] = block_terms(synced_ref[src], local_ref[src]).astype(BF16)


def terms_add_kernel(half_ref, synced_ref, local_ref, other_ref, out_ref):
    for start in range(0, out_ref.shape[-1], BLOCK):
        at = (0, slice(None), slice(start, start + BLOCK))
        src = (0, 0, slice(None), slice(start, start + BLOCK))
        terms = block_terms(synced_ref[src], local_ref[src])
        out_ref[at] = (terms + other_ref[at].astype(F32)).astype(BF16)


def half_terms(half, synced, local, other=None):
    groups, _, rows, width = synced.shape
    picked = pl.BlockSpec((1, 1, rows, width), lambda i, h: (i, h[0], 0, 0))
    plain = pl.BlockSpec((1, rows, width), lambda i, h: (i, 0, 0))
    operands = (synced, local) if other is None else (synced, local, other)
    count = groups * rows * width
    return pl.pallas_call(
        terms_kernel if other is None else terms_add_kernel,
        out_shape=jax.ShapeDtypeStruct((groups, rows, width), BF16),
        grid_spec=pltpu.PrefetchScalarGridSpec(
            num_scalar_prefetch=1,
            grid=(groups,),
            in_specs=[picked, picked] + [plain] * (len(operands) - 2),
            out_specs=plain,
        ),
        compiler_params=pltpu.CompilerParams(vmem_limit_bytes=16 << 20),
        cost_estimate=pl.CostEstimate(
            flops=12 * count, bytes_accessed=2 * count * (len(operands) + 1), transcendentals=0
        ),
        name="block_terms",
    )(half, *operands)


def back_kernel(own_ref, other_ref, cotangent_ref, gain_ref, out_ref):
    gain = gain_ref[...]
    for start in range(0, out_ref.shape[-1], HEAD):
        at = (slice(None), slice(start, start + HEAD))
        key = own_ref[at] + other_ref[at].astype(F32)
        pulled = cotangent_ref[at].astype(F32) * gain
        inv = lax.rsqrt(jnp.mean(key * key, axis=-1, keepdims=True) + NORM_EPSILON)
        along = jnp.mean(key * pulled, axis=-1, keepdims=True)
        out_ref[at] = (inv * pulled - key * (inv * inv * inv * along)).astype(BF16)


def head_back(own, other, cotangent, gain, start):
    rows, width = other.shape
    count = rows * width
    tile = 128
    spec = pl.BlockSpec((tile, width), lambda i: (i, 0))
    return pl.pallas_call(
        back_kernel,
        out_shape=jax.ShapeDtypeStruct((rows, width), BF16),
        grid=(rows // tile,),
        in_specs=[spec, spec, spec, pl.BlockSpec((1, HEAD), lambda i: (0, 0))],
        out_specs=spec,
        cost_estimate=pl.CostEstimate(
            flops=16 * count, bytes_accessed=10 * count, transcendentals=count // HEAD
        ),
        name="head_back",
    )(own, other, cotangent, gain)


def on_device(
    tokens,
    norm_gain,
    key_weight,
    key_gain,
    key_cotangent,
    local_fragment,
    synced_fragment,
    outer_momentum,
):
    c, x, yh = lax.axis_index("c"), lax.axis_index("x"), lax.axis_index("yh")
    y, z = lax.axis_index("yl"), lax.axis_index("z")
    weight = key_weight[0]
    depth, width = weight.shape
    cut = depth // 2

    low, high = weight[:cut], weight[cut:]
    with jax.named_scope("weight_gather"):
        prev_low, next_high = up(low, "z"), down(high, "z")
        prev_high, next_low = up(high, "z"), down(low, "z")
        far_low, far_high = up(prev_low, "z"), down(next_high, "z")

    def columns(values, half, step):
        start = (half * 4 + (z + step) % 4) * depth
        return lax.dynamic_slice_in_dim(values, start, depth, values.ndim - 1)

    order = (0, 1, 3, 2)
    with jax.named_scope("token_exchange"):
        theirs = [swap(columns(tokens, 1 - y, step), "yl") for step in order]
        floats = tokens.astype(F32)
        inv = lax.rsqrt(jnp.mean(floats * floats, axis=-1, keepdims=True) + NORM_EPSILON)
        their_inv = swap(inv.reshape(-1, 128), "yl").reshape(-1, 1)

    def normalize(values, scale, step):
        return (values.astype(F32) * scale * columns(norm_gain, y, step)).astype(BF16)

    with jax.named_scope("norm"):
        mine = {s: normalize(columns(tokens, y, s), inv, s) for s in order}
        other = {s: normalize(v, their_inv, s) for s, v in zip(order, theirs)}

    rows = outer_momentum.shape[0]
    frag = outer_momentum.shape[1]
    synced_groups = synced_fragment.reshape(8, 2, rows, frag)
    local_groups = local_fragment[0].reshape(8, 2, rows, frag)
    with jax.named_scope("fragment_sum"):
        sent = half_terms((1 - c).reshape(1), synced_groups, local_groups)
        pair = half_terms(c.reshape(1), synced_groups, local_groups, swap(sent, "c"))
        pair = pair.reshape(2, 4, rows, frag)

        def toward(step):
            return lax.dynamic_index_in_dim(pair, (x + step) % 4, 1, keepdims=False)

        ahead, behind, across, here = toward(1), toward(3), toward(2), toward(0)
        from_prev = up(jnp.stack([across[0], ahead[1]]), "x")
        from_next = down(jnp.stack([behind[0], across[1]]), "x")
        relay_up = up((ahead[0].astype(F32) + from_prev[0].astype(F32)).astype(BF16), "x")
        relay_down = down((behind[1].astype(F32) + from_next[1].astype(F32)).astype(BF16), "x")
        line = jnp.stack(
            [
                here[0].astype(F32) + from_next[0].astype(F32) + relay_up.astype(F32),
                here[1].astype(F32) + from_prev[1].astype(F32) + relay_down.astype(F32),
            ]
        )
        away = lax.dynamic_index_in_dim(line, 1 - yh, 0, keepdims=False).astype(BF16)
        own_sum = lax.dynamic_index_in_dim(line, yh, 0, keepdims=False) + swap(away, "yh").astype(F32)
    mean_delta = own_sum / 16
    new_momentum = MOMENTUM_DECAY * outer_momentum + mean_delta
    own_start = ((yh * 4 + x) * 2 + c) * rows
    own_synced = lax.dynamic_slice_in_dim(synced_fragment, own_start, rows, 0).astype(F32)
    own_new = (own_synced - OUTER_RATE * (mean_delta + MOMENTUM_DECAY * new_momentum)).astype(BF16)
    new_synced = lax.all_gather(own_new, REP, axis=0, tiled=True)

    def arrange(parts):
        return jnp.concatenate(
            [
                parts[0],
                parts[2][:, :cut],
                parts[1][:, cut:],
                parts[3][:, :cut],
                parts[2][:, cut:],
                parts[1][:, :cut],
                parts[3][:, cut:],
            ],
            axis=1,
        )

    mine, other = arrange(mine), arrange(other)
    weights = jnp.concatenate(
        [weight, far_low, next_high, prev_low, far_high, next_low, prev_high], axis=0
    )
    both = jnp.concatenate([mine, other], axis=0)
    own_keys = jnp.dot(mine, weights, preferred_element_type=F32)
    gain = key_gain.reshape(1, HEAD)

    pieces = []
    start = 0
    for size in CHUNKS:
        part = slice(start, start + size)
        start += size
        with jax.named_scope("keys"):
            partial = jnp.dot(other, weights[:, part], preferred_element_type=F32).astype(BF16)
            back = head_back(own_keys[:, part], swap(partial, "yl"), key_cotangent[:, part], gain, 0)
        with jax.named_scope("gradient"):
            backs = jnp.concatenate([back, swap(back, "yl")], axis=0)

            def grad(lo, hi):
                return lax.dot_general(
                    both[:, lo:hi], backs, (((0,), (0,)), ((), ())), preferred_element_type=F32
                )

            from_prev = up(grad(depth, 2 * depth).astype(BF16), "z")
            from_next = down(grad(2 * depth, 3 * depth).astype(BF16), "z")
            relay = grad(3 * depth, 4 * depth)
            here = grad(0, depth)
            relay_up = up((relay[:cut] + from_prev[:cut].astype(F32)).astype(BF16), "z")
            relay_down = down((relay[cut:] + from_next[cut:].astype(F32)).astype(BF16), "z")
            pieces.append(
                jnp.concatenate(
                    [
                        here[:cut] + from_next[:cut].astype(F32) + relay_up.astype(F32),
                        here[cut:] + from_prev[cut:].astype(F32) + relay_down.astype(F32),
                    ],
                    axis=0,
                ).astype(BF16)
            )
    key_gradient = jnp.concatenate(pieces, axis=1)[None]
    return (key_gradient, new_synced, new_momentum)


def solution(mesh):
    fine = Mesh(mesh.devices.reshape(2, 4, 2, 2, 4), AXES)
    return jax.shard_map(
        on_device,
        mesh=fine,
        in_specs=(
            P(AXES, None),
            P(),
            P(REP, FSDP, None),
            P(),
            P(AXES, None),
            P(REP, FSDP, None),
            P(FSDP, None),
            P(FSDP + REP, None),
        ),
        out_specs=(P(REP, FSDP, None), P(FSDP, None), P(FSDP + REP, None)),
        check_vma=False,
    )
```

```python
import jax
import jax.numpy as jnp
from jax import lax
from jax.experimental import pallas as pl
from jax.experimental.pallas import tpu as pltpu
from jax.sharding import Mesh, PartitionSpec as P

BLOCK = 128
HEAD = 128

NORM_EPSILON = 1e-05
SCALE_EPSILON = 1e-06
OUTER_RATE = 0.7
MOMENTUM_DECAY = 0.9

AXES = ("yh", "x", "c", "yl", "z")
REP = ("yh", "x", "c")
FSDP = ("yl", "z")
CHUNKS = (256, 256, 256, 256)

F32 = jnp.float32
BF16 = jnp.bfloat16


def shift(value, axis, size, step):
    return lax.ppermute(value, axis, [(i, (i + step) % size) for i in range(size)])


def up(value, axis):
    return shift(value, axis, 4, 1)


def down(value, axis):
    return shift(value, axis, 4, 3)


def swap(value, axis):
    return shift(value, axis, 2, 1)


def block_terms(synced, local):
    delta = synced.astype(F32) - local.astype(F32)
    top = jnp.max(jnp.abs(delta), axis=-1, keepdims=True)
    scale = (top + SCALE_EPSILON).astype(BF16).astype(F32)
    level = (delta / scale).astype(BF16).astype(F32)
    return level * scale


def terms_kernel(pick, synced_ref, local_ref, *refs):
    out_ref = refs[-1]
    for group in range(out_ref.shape[0]):
        for start in range(0, out_ref.shape[-1], BLOCK):
            at = (group, slice(None), slice(start, start + BLOCK))
            src = (0, group, 0, slice(None), slice(start, start + BLOCK))
            terms = block_terms(synced_ref[src], local_ref[src])
            if len(refs) > 1:
                terms = terms + refs[0][at].astype(F32)
            out_ref[at] = terms.astype(BF16)


def half_terms(half, core, synced, local, other=None):
    _, groups, _, rows, width = synced.shape
    block = 2
    picked = pl.BlockSpec((1, block, 1, rows, width), lambda i, p: (half, i, p[0], 0, 0))
    plain = pl.BlockSpec((block, rows, width), lambda i, p: (i, 0, 0))
    operands = (synced, local) if other is None else (synced, local, other)
    count = groups * rows * width
    return pl.pallas_call(
        terms_kernel,
        out_shape=jax.ShapeDtypeStruct((groups, rows, width), BF16),
        grid_spec=pltpu.PrefetchScalarGridSpec(
            num_scalar_prefetch=1,
            grid=(groups // block,),
            in_specs=[picked, picked] + [plain] * (len(operands) - 2),
            out_specs=plain,
        ),
        compiler_params=pltpu.CompilerParams(vmem_limit_bytes=56 << 20),
        cost_estimate=pl.CostEstimate(
            flops=12 * count, bytes_accessed=2 * count * (len(operands) + 1), transcendentals=0
        ),
        name="block_terms",
    )(core.reshape(1), *operands)


def keys_kernel(tokens_ref, weight_ref, first_ref, out_ref, total):
    step = pl.program_id(0)
    part = jnp.dot(tokens_ref[...], weight_ref[...], preferred_element_type=F32)

    @pl.when(step == 0)
    def _():
        total[...] = part

    @pl.when(step > 0)
    def _():
        total[...] += part

    @pl.when(step == pl.num_programs(0) - 1)
    def _():
        rows = first_ref.shape[0]
        out_ref[:rows] = first_ref[...]
        out_ref[rows:] = total[...].astype(BF16)


def partial_keys(tokens, weights, first, start, size):
    rows, depth = tokens.shape
    block = depth // 3
    return pl.pallas_call(
        keys_kernel,
        out_shape=jax.ShapeDtypeStruct((2 * rows, size), BF16),
        grid=(3,),
        in_specs=[
            pl.BlockSpec((rows, block), lambda i: (0, i)),
            pl.BlockSpec((block, size), lambda i: (i, start // size)),
            pl.BlockSpec((rows, size), lambda i: (0, start // size)),
        ],
        out_specs=pl.BlockSpec((2 * rows, size), lambda i: (0, 0)),
        scratch_shapes=[pltpu.VMEM((rows, size), F32)],
        compiler_params=pltpu.CompilerParams(vmem_limit_bytes=8 << 20),
        cost_estimate=pl.CostEstimate(
            flops=2 * rows * depth * size,
            bytes_accessed=2 * (rows * depth + depth * size + 3 * rows * size),
            transcendentals=0,
        ),
        name="partial_keys",
    )(tokens, weights, first)


def back_kernel(own_ref, other_ref, cotangent_ref, gain_ref, inv_ref, out_ref):
    gain = gain_ref[...]
    token_inv = inv_ref[...]
    for start in range(0, out_ref.shape[-1], HEAD):
        at = (slice(None), slice(start, start + HEAD))
        key = (own_ref[at] + other_ref[at].astype(F32)) * token_inv
        pulled = cotangent_ref[at].astype(F32) * gain
        inv = lax.rsqrt(jnp.mean(key * key, axis=-1, keepdims=True) + NORM_EPSILON)
        along = jnp.mean(key * pulled, axis=-1, keepdims=True)
        back = inv * pulled - key * (inv * inv * inv * along)
        out_ref[at] = (back * token_inv).astype(BF16)


def head_back(own, other, cotangent, gain, inv, start):
    rows, width = other.shape
    count = rows * width
    at = pl.BlockSpec((rows, width), lambda i: (0, start // width))
    spec = pl.BlockSpec((rows, width), lambda i: (0, 0))
    return pl.pallas_call(
        back_kernel,
        out_shape=jax.ShapeDtypeStruct((rows, width), BF16),
        grid=(1,),
        in_specs=[
            at,
            spec,
            at,
            pl.BlockSpec((1, HEAD), lambda i: (0, 0)),
            pl.BlockSpec((rows, 1), lambda i: (0, 0)),
        ],
        out_specs=spec,
        compiler_params=pltpu.CompilerParams(vmem_limit_bytes=10 << 20),
        cost_estimate=pl.CostEstimate(
            flops=16 * count, bytes_accessed=10 * count, transcendentals=count // HEAD
        ),
        name="head_back",
    )(own, other, cotangent, gain, inv)


def final_kernel(own_ref, prev_ref, next_ref, up_ref, down_ref, gain_ref, *rest):
    out_ref = rest[-1]
    cut = up_ref.shape[0]
    low, high = slice(0, cut), slice(cut, 2 * cut)
    whole = own_ref[low] + next_ref[...].astype(F32) + up_ref[...].astype(F32)
    out_ref[low] = (whole * gain_ref[low]).astype(BF16)
    whole = own_ref[high] + prev_ref[...].astype(F32) + down_ref[...].astype(F32)
    out_ref[high] = (whole * gain_ref[high]).astype(BF16)


def finish(own, from_prev, from_next, relay_up, relay_down, gain, out, start, total):
    depth, width = own.shape
    operands = [own, from_prev, from_next, relay_up, relay_down, gain]
    specs = [pl.BlockSpec(value.shape, lambda i: (0, 0)) for value in operands]
    aliases = {}
    if out is not None:
        operands, specs = operands + [out], specs + [pl.BlockSpec(memory_space=pl.ANY)]
        aliases = {6: 0}
    return pl.pallas_call(
        final_kernel,
        out_shape=jax.ShapeDtypeStruct((depth, total), BF16),
        grid=(1,),
        in_specs=specs,
        out_specs=pl.BlockSpec((depth, width), lambda i: (0, start // width)),
        input_output_aliases=aliases,
        compiler_params=pltpu.CompilerParams(vmem_limit_bytes=10 << 20),
        cost_estimate=pl.CostEstimate(
            flops=4 * depth * width, bytes_accessed=12 * depth * width, transcendentals=0
        ),
        name="gradient_final",
    )(*operands)


def place_kernel(where, own_ref, other_ref, out_ref):
    for core in range(2):
        mine = where[0] == core

        @pl.when(mine)
        def _():
            out_ref[:, 0, core] = own_ref[0]

        @pl.when(jnp.logical_not(mine))
        def _():
            out_ref[:, 0, core] = other_ref[0]


def place(c, own, other):
    _, _, rows, width = own.shape
    source = pl.BlockSpec((1, 2, rows, width), lambda i, w: (i, 0, 0, 0))
    out = pl.pallas_call(
        place_kernel,
        out_shape=jax.ShapeDtypeStruct((2, 4, 2, rows, width), BF16),
        grid_spec=pltpu.PrefetchScalarGridSpec(
            num_scalar_prefetch=1,
            grid=(4,),
            in_specs=[source, source],
            out_specs=pl.BlockSpec((2, 1, 2, rows, width), lambda i, w: (0, i, 0, 0, 0)),
        ),
        compiler_params=pltpu.CompilerParams(vmem_limit_bytes=10 << 20),
        cost_estimate=pl.CostEstimate(
            flops=0, bytes_accessed=64 * rows * width, transcendentals=0
        ),
        name="place_rows",
    )(c.reshape(1), own, other)
    return out.reshape(16 * rows, width)


def columns_kernel(half, in_ref, out_ref):
    out_ref[...] = in_ref[...]


def columns(tokens, half, part):
    rows, width = tokens.shape[0] // 2, tokens.shape[1] // 2
    tile = rows // 2
    steps = rows // tile
    return pl.pallas_call(
        columns_kernel,
        out_shape=jax.ShapeDtypeStruct((rows, width), tokens.dtype),
        grid_spec=pltpu.PrefetchScalarGridSpec(
            num_scalar_prefetch=1,
            grid=(rows // tile,),
            in_specs=[pl.BlockSpec((tile, width), lambda i, p: (part * steps + i, p[0]))],
            out_specs=pl.BlockSpec((tile, width), lambda i, p: (i, 0)),
        ),
        compiler_params=pltpu.CompilerParams(vmem_limit_bytes=56 << 20),
        cost_estimate=pl.CostEstimate(
            flops=0, bytes_accessed=4 * rows * width, transcendentals=0
        ),
        name="token_columns",
    )(half.reshape(1), tokens)


def columns_norm_kernel(half, in_ref, out_ref, inv_ref):
    width = out_ref.shape[1]
    floats = in_ref[...].astype(F32)
    mean_sq = jnp.mean(floats * floats, axis=-1, keepdims=True)
    inv_ref[...] = lax.rsqrt(mean_sq + NORM_EPSILON)

    @pl.when(half[0] == 0)
    def _():
        out_ref[...] = in_ref[:, :width]

    @pl.when(half[0] == 1)
    def _():
        out_ref[...] = in_ref[:, width:]


def columns_norm(tokens, half):
    rows, width = tokens.shape[0], tokens.shape[1] // 2
    tile = rows // 8
    return pl.pallas_call(
        columns_norm_kernel,
        out_shape=(
            jax.ShapeDtypeStruct((rows, width), tokens.dtype),
            jax.ShapeDtypeStruct((rows, 1), F32),
        ),
        grid_spec=pltpu.PrefetchScalarGridSpec(
            num_scalar_prefetch=1,
            grid=(rows // tile,),
            in_specs=[pl.BlockSpec((tile, 2 * width), lambda i, p: (i, 0))],
            out_specs=(
                pl.BlockSpec((tile, width), lambda i, p: (i, 0)),
                pl.BlockSpec((tile, 1), lambda i, p: (i, 0)),
            ),
        ),
        compiler_params=pltpu.CompilerParams(vmem_limit_bytes=56 << 20),
        cost_estimate=pl.CostEstimate(
            flops=4 * rows * width, bytes_accessed=6 * rows * width, transcendentals=rows
        ),
        name="token_norm",
    )(half.reshape(1), tokens)


def tie(*values):
    return lax.optimization_barrier(values)


def on_device(
    tokens,
    norm_gain,
    key_weight,
    key_gain,
    key_cotangent,
    local_fragment,
    synced_fragment,
    outer_momentum,
):
    c, x, yh = lax.axis_index("c"), lax.axis_index("x"), lax.axis_index("yh")
    y, z = lax.axis_index("yl"), lax.axis_index("z")
    depth, width = key_weight.shape[1:]
    cut = depth // 2

    with jax.named_scope("token_exchange"):
        sent = [columns(tokens, 1 - y, part) for part in range(2)]
        sent[0], local_fragment = tie(sent[0], local_fragment)
        first = swap(sent[0], "yl")
        sent[1], first = tie(sent[1], first)
        others = (first, swap(sent[1], "yl"))

    with jax.named_scope("weight_gather"):
        row_gain = lax.dynamic_slice_in_dim(norm_gain, (y * 4 + z) * depth, depth, 0).reshape(-1, 1)
        scaled = (key_weight[0].astype(F32) * row_gain).astype(BF16)
        weights = lax.all_gather(scaled, "z", axis=0, tiled=True)

    with jax.named_scope("token_norm"):
        mine, inv = columns_norm(tokens, y)

    rows = outer_momentum.shape[0]
    frag = outer_momentum.shape[1]
    with jax.named_scope("fragment_sum"):
        groups = [v.reshape(2, 4, 2, rows, frag) for v in (synced_fragment, local_fragment[0])]
        parts = [half_terms(h, 1 - c, *groups) for h in range(2)]
        pair = [half_terms(h, c, *groups, swap(parts[h], "c")) for h in range(2)]

        def toward(h, step):
            return lax.dynamic_index_in_dim(pair[h], (x + step) % 4, 0, keepdims=False)

        from_prev = up(jnp.stack([toward(0, 2), toward(1, 1)]), "x")
        from_next = down(jnp.stack([toward(0, 3), toward(1, 2)]), "x")
        relay_up = up((toward(0, 1).astype(F32) + from_prev[0].astype(F32)).astype(BF16), "x")
        relay_down = down((toward(1, 3).astype(F32) + from_next[1].astype(F32)).astype(BF16), "x")

    with jax.named_scope("keys"):
        first = jnp.dot(others[0], weights, preferred_element_type=F32).astype(BF16)
        own_keys = jnp.dot(mine, weights, preferred_element_type=F32)
    relay_up, relay_down, weights, first, own_keys, others = tie(
        relay_up, relay_down, weights, first, own_keys, others
    )

    with jax.named_scope("fragment_sum"):
        line = jnp.stack(
            [
                toward(0, 0).astype(F32) + from_next[0].astype(F32) + relay_up.astype(F32),
                toward(1, 0).astype(F32) + from_prev[1].astype(F32) + relay_down.astype(F32),
            ]
        )
        away = lax.dynamic_index_in_dim(line, 1 - yh, 0, keepdims=False).astype(BF16)
        away = swap(away, "yh")

    with jax.named_scope("keys"):
        starts = [sum(CHUNKS[:i]) for i in range(len(CHUNKS))]

    def outer_step(away):
        own_sum = lax.dynamic_index_in_dim(line, yh, 0, keepdims=False) + away.astype(F32)
        mean_delta = own_sum / 16
        new_momentum = MOMENTUM_DECAY * outer_momentum + mean_delta
        own_start = ((yh * 4 + x) * 2 + c) * rows
        own_synced = lax.dynamic_slice_in_dim(synced_fragment, own_start, rows, 0).astype(F32)
        own_new = (own_synced - OUTER_RATE * (mean_delta + MOMENTUM_DECAY * new_momentum)).astype(BF16)
        return own_new, new_momentum

    def gather(own_new, far_new):
        here = jnp.where(yh == 0, jnp.stack([own_new, far_new]), jnp.stack([far_new, own_new]))
        return lax.all_gather(here, "x")

    gain = key_gain.reshape(1, HEAD)
    contract = (((0,), (0,)), ((), ()))
    count = len(CHUNKS)
    arrived = [None] * count
    with jax.named_scope("keys"):
        second = others[1]
        for step in range(min(2, count)):
            partial = partial_keys(second, weights, first, starts[step], CHUNKS[step])
            arrived[step] = swap(partial, "yl")
        second, arrived[0] = tie(second, arrived[0])
        partial = [
            partial_keys(second, weights, first, starts[step], CHUNKS[step]) if step >= 2 else None
            for step in range(count)
        ]

    totals, came, sends = [], [], []
    out = None
    for step in range(count + 2):
        if step < count:
            start, size = starts[step], CHUNKS[step]
            with jax.named_scope("keys"):
                if step == 2:
                    arrived[step], away = tie(arrived[step], away)
                back = head_back(own_keys, arrived[step], key_cotangent, gain, inv, start)
                if step >= 1:
                    back, totals[-1] = tie(back, totals[-1])
                if step == 3:
                    back, *held = tie(back, *came[0])
                    came[0] = held
                other_back = swap(back, "yl")
                if step + 2 < count:
                    held, back = tie(partial[step + 2], back)
                    arrived[step + 2] = swap(held, "yl")
                if step == 2:
                    own_new, new_momentum = outer_step(away)
                    held, back = tie(own_new, back)
                    far_new = swap(held, "yh")
                if step == 3:
                    other_back, far_new = tie(other_back, far_new)
            with jax.named_scope("gradient"):
                total = lax.dot_general(mine, back, contract, preferred_element_type=F32)
                tile = other_back.shape[0] // 2
                for part in range(2):
                    total = total + lax.dot_general(
                        others[part],
                        other_back[part * tile : (part + 1) * tile],
                        contract,
                        preferred_element_type=F32,
                    )
                totals.append(total)

        def rows_of(total, away, part):
            place = (z + away) % 4 * depth + part * cut
            return lax.dynamic_slice_in_dim(total, place, cut, 0)

        with jax.named_scope("gradient"):
            to_next, to_prev = [], []
            if step < count:
                to_next += [rows_of(totals[step], 2, 0), rows_of(totals[step], 1, 1)]
                to_prev += [rows_of(totals[step], 2, 1), rows_of(totals[step], 3, 0)]
            if step >= 2:
                total, (from_prev, from_next) = totals[step - 2], came[step - 2]
                relay_up = rows_of(total, 1, 0) + from_prev[:cut].astype(F32)
                relay_down = rows_of(total, 3, 1) + from_next[:cut].astype(F32)
                if step < count:
                    relay_up = jnp.pad(relay_up, ((0, 0), (0, CHUNKS[step] - relay_up.shape[1])))
                    relay_down = jnp.pad(
                        relay_down, ((0, 0), (0, CHUNKS[step] - relay_down.shape[1]))
                    )
                to_next.append(relay_up)
                to_prev.append(relay_down)
            to_next = jnp.concatenate([v.astype(BF16) for v in to_next], axis=0)
            to_prev = jnp.concatenate([v.astype(BF16) for v in to_prev], axis=0)
            sends.append((to_next, to_prev))
            came.append((up(to_next, "z"), down(to_prev, "z")))
            if step == count - 1:
                line = gather(own_new, far_new)
            if step == count + 1:
                line, last, *held = tie(line, out, *came[step])
                came[step], out = held, last
            if step >= 2:
                total, size = totals[step - 2], CHUNKS[step - 2]
                from_prev, from_next = came[step - 2]
                relay_up, relay_down = (v[-cut:, :size] for v in came[step])
                own = lax.dynamic_slice_in_dim(total, z * depth, depth, 0)
                out = finish(
                    own,
                    from_prev[cut : 2 * cut],
                    from_next[cut : 2 * cut],
                    relay_up,
                    relay_down,
                    row_gain,
                    out,
                    starts[step - 2],
                    width,
                )
    with jax.named_scope("fragment_gather"):
        new_synced = place(c, line, swap(line, "c"))
    return (out[None], new_synced, new_momentum)


def solution(mesh):
    fine = Mesh(mesh.devices.reshape(2, 4, 2, 2, 4), AXES)
    return jax.shard_map(
        on_device,
        mesh=fine,
        in_specs=(
            P(AXES, None),
            P(),
            P(REP, FSDP, None),
            P(),
            P(AXES, None),
            P(REP, FSDP, None),
            P(FSDP, None),
            P(FSDP + REP, None),
        ),
        out_specs=(P(REP, FSDP, None), P(FSDP, None), P(FSDP + REP, None)),
        check_vma=False,
    )
```

```python
import functools

import jax
import jax.numpy as jnp
from jax import lax
from jax.experimental import pallas as pl
from jax.experimental.pallas import tpu as pltpu
from jax.sharding import Mesh, PartitionSpec as P

BLOCK = 128
HEAD = 128

NORM_EPSILON = 1e-05
SCALE_EPSILON = 1e-06
OUTER_RATE = 0.7
MOMENTUM_DECAY = 0.9

AXES = ("yh", "x", "c", "yl", "z")
REP = ("yh", "x", "c")
FSDP = ("yl", "z")
CHUNKS = (256, 256, 256, 256)

F32 = jnp.float32
BF16 = jnp.bfloat16


def shift(value, axis, size, step):
    return lax.ppermute(value, axis, [(i, (i + step) % size) for i in range(size)])


def up(value, axis):
    return shift(value, axis, 4, 1)


def down(value, axis):
    return shift(value, axis, 4, 3)


def swap(value, axis):
    return shift(value, axis, 2, 1)


def block_terms(synced, local):
    delta = synced.astype(F32) - local.astype(F32)
    top = jnp.max(jnp.abs(delta), axis=-1, keepdims=True)
    scale = (top + SCALE_EPSILON).astype(BF16).astype(F32)
    level = (delta / scale).astype(BF16).astype(F32)
    return level * scale


def terms_kernel(pick, synced_ref, local_ref, *refs):
    out_ref = refs[-1]
    for group in range(out_ref.shape[0]):
        for start in range(0, out_ref.shape[-1], BLOCK):
            at = (group, slice(None), slice(start, start + BLOCK))
            src = (0, group, 0, slice(None), slice(start, start + BLOCK))
            terms = block_terms(synced_ref[src], local_ref[src])
            if len(refs) > 1:
                terms = terms + refs[0][at].astype(F32)
            out_ref[at] = terms.astype(BF16)


def half_terms(half, core, synced, local, other=None):
    _, groups, _, rows, width = synced.shape
    block = 2
    picked = pl.BlockSpec((1, block, 1, rows, width), lambda i, p: (half, i, p[0], 0, 0))
    plain = pl.BlockSpec((block, rows, width), lambda i, p: (i, 0, 0))
    operands = (synced, local) if other is None else (synced, local, other)
    count = groups * rows * width
    return pl.pallas_call(
        terms_kernel,
        out_shape=jax.ShapeDtypeStruct((groups, rows, width), BF16),
        grid_spec=pltpu.PrefetchScalarGridSpec(
            num_scalar_prefetch=1,
            grid=(groups // block,),
            in_specs=[picked, picked] + [plain] * (len(operands) - 2),
            out_specs=plain,
        ),
        compiler_params=pltpu.CompilerParams(vmem_limit_bytes=56 << 20),
        cost_estimate=pl.CostEstimate(
            flops=12 * count, bytes_accessed=2 * count * (len(operands) + 1), transcendentals=0
        ),
        name="block_terms",
    )(core.reshape(1), *operands)


def keys_kernel(tokens_ref, weight_ref, *refs):
    out_ref, total = refs[-2:]
    step = pl.program_id(0)
    part = jnp.dot(tokens_ref[...], weight_ref[...], preferred_element_type=F32)

    @pl.when(step == 0)
    def _():
        total[...] = part

    @pl.when(step > 0)
    def _():
        total[...] += part

    @pl.when(step == pl.num_programs(0) - 1)
    def _():
        if len(refs) == 2:
            out_ref[...] = total[...].astype(out_ref.dtype)
        else:
            rows = refs[0].shape[0]
            out_ref[:rows] = refs[0][...]
            out_ref[rows:] = total[...].astype(BF16)


def chunk_keys(tokens, weights, start, size, dtype, first=None):
    rows, depth = tokens.shape
    steps = 2 if size < weights.shape[1] else 4
    block = depth // steps
    specs = [
        pl.BlockSpec((rows, block), lambda i: (0, i)),
        pl.BlockSpec((block, size), lambda i: (i, start // size)),
    ]
    operands = [tokens, weights]
    shape = jax.ShapeDtypeStruct((rows, size), dtype)
    if first is not None:
        specs.append(pl.BlockSpec((rows, size), lambda i: (0, start // size)))
        operands.append(first)
        shape = jax.ShapeDtypeStruct((2 * rows, size), dtype)
    return pl.pallas_call(
        keys_kernel,
        out_shape=shape,
        grid=(steps,),
        in_specs=specs,
        out_specs=pl.BlockSpec(shape.shape, lambda i: (0, 0)),
        scratch_shapes=[pltpu.VMEM((rows, size), F32)],
        compiler_params=pltpu.CompilerParams(vmem_limit_bytes=20 << 20),
        cost_estimate=pl.CostEstimate(
            flops=2 * rows * depth * size,
            bytes_accessed=2 * (rows * depth + depth * size + 3 * rows * size),
            transcendentals=0,
        ),
        name="chunk_keys",
    )(*operands)


def back_kernel(own_ref, other_ref, cotangent_ref, gain_ref, inv_ref, out_ref):
    gain = gain_ref[...]
    token_inv = inv_ref[...]
    for start in range(0, out_ref.shape[-1], HEAD):
        at = (slice(None), slice(start, start + HEAD))
        key = (own_ref[at] + other_ref[at].astype(F32)) * token_inv
        pulled = cotangent_ref[at].astype(F32) * gain
        inv = lax.rsqrt(jnp.mean(key * key, axis=-1, keepdims=True) + NORM_EPSILON)
        along = jnp.mean(key * pulled, axis=-1, keepdims=True)
        back = inv * pulled - key * (inv * inv * inv * along)
        out_ref[at] = (back * token_inv).astype(BF16)


def head_back(own, other, cotangent, gain, inv, start):
    rows, width = other.shape
    count = rows * width
    at = pl.BlockSpec((rows, width), lambda i: (0, start // width))
    spec = pl.BlockSpec((rows, width), lambda i: (0, 0))
    return pl.pallas_call(
        back_kernel,
        out_shape=jax.ShapeDtypeStruct((rows, width), BF16),
        grid=(1,),
        in_specs=[
            at,
            spec,
            at,
            pl.BlockSpec((1, HEAD), lambda i: (0, 0)),
            pl.BlockSpec((rows, 1), lambda i: (0, 0)),
        ],
        out_specs=spec,
        compiler_params=pltpu.CompilerParams(vmem_limit_bytes=10 << 20),
        cost_estimate=pl.CostEstimate(
            flops=16 * count, bytes_accessed=10 * count, transcendentals=count // HEAD
        ),
        name="head_back",
    )(own, other, cotangent, gain, inv)


def payload_kernel(*refs, fresh, relayed):
    ins, outs = refs[:-2], refs[-2:]
    cut = outs[0].shape[0] // (2 * fresh + relayed)
    for side, out_ref in enumerate(outs):
        if fresh:
            out_ref[:cut] = ins[2 * side][...]
            out_ref[cut : 2 * cut] = ins[2 * side + 1][...]
        if relayed:
            total, arrived = ins[4 * fresh + 2 * side], ins[4 * fresh + 2 * side + 1]
            out_ref[2 * cut * fresh :] = (total[...].astype(F32) + arrived[...].astype(F32)).astype(BF16)


HALVES = (4, 7, 5, 2, 6, 3)


def payload(total, before, came):
    source = total if total is not None else before
    cut, width = source.shape[0] // 8, source.shape[1]
    fresh, relayed = int(total is not None), int(before is not None)
    operands, specs = [], []

    def block(value, slot):
        operands.append(value)
        specs.append(pl.BlockSpec((cut, width), lambda i: (HALVES[slot], 0)))

    if fresh:
        for slot in range(4):
            block(total, slot)
    if relayed:
        for side in range(2):
            block(before, 4 + side)
            operands.append(came[side])
            specs.append(pl.BlockSpec((cut, width), lambda i: (0, 0)))
    shape = jax.ShapeDtypeStruct(((2 * fresh + relayed) * cut, width), BF16)
    out_spec = pl.BlockSpec(shape.shape, lambda i: (0, 0))
    return pl.pallas_call(
        functools.partial(payload_kernel, fresh=fresh, relayed=relayed),
        out_shape=(shape, shape),
        grid=(1,),
        in_specs=specs,
        out_specs=(out_spec, out_spec),
        compiler_params=pltpu.CompilerParams(vmem_limit_bytes=10 << 20),
        cost_estimate=pl.CostEstimate(
            flops=4 * cut * width, bytes_accessed=30 * cut * width, transcendentals=0
        ),
        name="gradient_payload",
    )(*operands)


def final_kernel(own_ref, prev_ref, next_ref, up_ref, down_ref, *rest):
    out_ref = rest[-1]
    cut = up_ref.shape[0]
    low, high = slice(0, cut), slice(cut, 2 * cut)
    out_ref[low] = (
        own_ref[low].astype(F32) + next_ref[...].astype(F32) + up_ref[...].astype(F32)
    ).astype(BF16)
    out_ref[high] = (
        own_ref[high].astype(F32) + prev_ref[...].astype(F32) + down_ref[...].astype(F32)
    ).astype(BF16)


def finish(total, came, relayed, out, start, width):
    size = total.shape[1]
    depth = total.shape[0] // 4
    cut = depth // 2
    last = relayed[0].shape[0] // cut - 1
    one = pl.BlockSpec((cut, size), lambda i: (1, 0))
    end = pl.BlockSpec((cut, size), lambda i: (last, 0))
    operands = [total, *came, *relayed]
    specs = [pl.BlockSpec((depth, size), lambda i: (0, 0)), one, one, end, end]
    aliases = {}
    if out is not None:
        operands, specs = operands + [out], specs + [pl.BlockSpec(memory_space=pl.ANY)]
        aliases = {5: 0}
    return pl.pallas_call(
        final_kernel,
        out_shape=jax.ShapeDtypeStruct((depth, width), BF16),
        grid=(1,),
        in_specs=specs,
        out_specs=pl.BlockSpec((depth, size), lambda i: (0, start // size)),
        input_output_aliases=aliases,
        compiler_params=pltpu.CompilerParams(vmem_limit_bytes=10 << 20),
        cost_estimate=pl.CostEstimate(
            flops=4 * depth * size, bytes_accessed=12 * depth * size, transcendentals=0
        ),
        name="gradient_final",
    )(*operands)


def place_kernel(where, own_ref, other_ref, out_ref):
    for core in range(2):
        mine = where[0] == core

        @pl.when(mine)
        def _():
            out_ref[:, 0, core] = own_ref[0]

        @pl.when(jnp.logical_not(mine))
        def _():
            out_ref[:, 0, core] = other_ref[0]


def place(x, c, own, other):
    _, _, rows, width = own.shape
    source = pl.BlockSpec((1, 2, rows, width), lambda i, w: ((i + 4 - w[1]) % 4, 0, 0, 0))
    out = pl.pallas_call(
        place_kernel,
        out_shape=jax.ShapeDtypeStruct((2, 4, 2, rows, width), BF16),
        grid_spec=pltpu.PrefetchScalarGridSpec(
            num_scalar_prefetch=1,
            grid=(4,),
            in_specs=[source, source],
            out_specs=pl.BlockSpec((2, 1, 2, rows, width), lambda i, w: (0, i, 0, 0, 0)),
        ),
        compiler_params=pltpu.CompilerParams(vmem_limit_bytes=10 << 20),
        cost_estimate=pl.CostEstimate(
            flops=0, bytes_accessed=64 * rows * width, transcendentals=0
        ),
        name="place_rows",
    )(jnp.stack([c, x]).astype(jnp.int32), own, other)
    return out.reshape(16 * rows, width)


def arrange(values_ref, gain_ref, out_ref, z, base):
    width = out_ref.shape[1] // 4
    for slot in range(4):
        start = base + lax.rem(z + 4 - slot, 4) * width
        at = (slice(None), pl.ds(pl.multiple_of(start, width), width))
        out_ref[:, slot * width : (slot + 1) * width] = (
            values_ref[at].astype(F32) * gain_ref[at]
        ).astype(BF16)


def columns_kernel(place, in_ref, gain_ref, out_ref):
    arrange(in_ref, gain_ref, out_ref, place[1], 0)


def columns(tokens, gain, place, part):
    rows, width = tokens.shape[0] // 2, tokens.shape[1] // 2
    tile = rows // 2
    return pl.pallas_call(
        columns_kernel,
        out_shape=jax.ShapeDtypeStruct((rows, width), tokens.dtype),
        grid_spec=pltpu.PrefetchScalarGridSpec(
            num_scalar_prefetch=1,
            grid=(2,),
            in_specs=[
                pl.BlockSpec((tile, width), lambda i, p: (part * 2 + i, 1 - p[0])),
                pl.BlockSpec((1, width), lambda i, p: (0, 1 - p[0])),
            ],
            out_specs=pl.BlockSpec((tile, width), lambda i, p: (i, 0)),
        ),
        compiler_params=pltpu.CompilerParams(vmem_limit_bytes=56 << 20),
        cost_estimate=pl.CostEstimate(
            flops=0, bytes_accessed=4 * rows * width, transcendentals=0
        ),
        name="token_columns",
    )(place, tokens, gain)


def columns_norm_kernel(place, in_ref, gain_ref, out_ref, inv_ref):
    floats = in_ref[...].astype(F32)
    mean_sq = jnp.mean(floats * floats, axis=-1, keepdims=True)
    inv_ref[...] = lax.rsqrt(mean_sq + NORM_EPSILON)
    arrange(in_ref, gain_ref, out_ref, place[1], place[0] * out_ref.shape[1])


def columns_norm(tokens, gain, place):
    rows, width = tokens.shape[0], tokens.shape[1] // 2
    tile = rows // 8
    return pl.pallas_call(
        columns_norm_kernel,
        out_shape=(
            jax.ShapeDtypeStruct((rows, width), tokens.dtype),
            jax.ShapeDtypeStruct((rows, 1), F32),
        ),
        grid_spec=pltpu.PrefetchScalarGridSpec(
            num_scalar_prefetch=1,
            grid=(rows // tile,),
            in_specs=[
                pl.BlockSpec((tile, 2 * width), lambda i, p: (i, 0)),
                pl.BlockSpec((1, 2 * width), lambda i, p: (0, 0)),
            ],
            out_specs=(
                pl.BlockSpec((tile, width), lambda i, p: (i, 0)),
                pl.BlockSpec((tile, 1), lambda i, p: (i, 0)),
            ),
        ),
        compiler_params=pltpu.CompilerParams(vmem_limit_bytes=56 << 20),
        cost_estimate=pl.CostEstimate(
            flops=4 * rows * width, bytes_accessed=6 * rows * width, transcendentals=rows
        ),
        name="token_norm",
    )(place, tokens, gain)


def tie(*values):
    return lax.optimization_barrier(values)


def on_device(
    tokens,
    norm_gain,
    key_weight,
    key_gain,
    key_cotangent,
    local_fragment,
    synced_fragment,
    outer_momentum,
):
    c, x, yh = lax.axis_index("c"), lax.axis_index("x"), lax.axis_index("yh")
    y, z = lax.axis_index("yl"), lax.axis_index("z")
    depth, width = key_weight.shape[1:]
    cut = depth // 2

    spot = jnp.stack([y, z]).astype(jnp.int32)

    token_gain = norm_gain.reshape(1, -1)
    with jax.named_scope("token_exchange"):
        sent = [columns(tokens, token_gain, spot, part) for part in range(2)]
        sent[0], local_fragment = tie(sent[0], local_fragment)
        first = swap(sent[0], "yl")
        sent[1], first = tie(sent[1], first)
        others = (first, swap(sent[1], "yl"))

    with jax.named_scope("weight_gather"):
        weight = key_weight[0]
        cut = weight.shape[0] // 2
        prev, following = up(weight, "z"), down(weight, "z")
        far = [up(prev[:cut], "z"), down(following[cut:], "z")]
        weights = jnp.concatenate([weight, prev, *far, following], axis=0)

    with jax.named_scope("token_norm"):
        mine, inv = columns_norm(tokens, token_gain, spot)

    rows = outer_momentum.shape[0]
    frag = outer_momentum.shape[1]
    with jax.named_scope("fragment_sum"):
        groups = [v.reshape(2, 4, 2, rows, frag) for v in (synced_fragment, local_fragment[0])]
        parts = [half_terms(h, 1 - c, *groups) for h in range(2)]
        pair = [half_terms(h, c, *groups, swap(parts[h], "c")) for h in range(2)]

        def toward(h, step):
            return lax.dynamic_index_in_dim(pair[h], (x + step) % 4, 0, keepdims=False)

        from_prev = up(jnp.stack([toward(0, 2), toward(1, 1)]), "x")
        from_next = down(jnp.stack([toward(0, 3), toward(1, 2)]), "x")

    with jax.named_scope("keys"):
        first = chunk_keys(others[0], weights, 0, width, BF16)
        own_keys = chunk_keys(mine, weights, 0, width, F32)
    from_prev, from_next, *others = tie(from_prev, from_next, *others)

    with jax.named_scope("fragment_sum"):
        relay_up = up((toward(0, 1).astype(F32) + from_prev[0].astype(F32)).astype(BF16), "x")
        relay_down = down((toward(1, 3).astype(F32) + from_next[1].astype(F32)).astype(BF16), "x")
        line = jnp.stack(
            [
                toward(0, 0).astype(F32) + from_next[0].astype(F32) + relay_up.astype(F32),
                toward(1, 0).astype(F32) + from_prev[1].astype(F32) + relay_down.astype(F32),
            ]
        )
        away = lax.dynamic_index_in_dim(line, 1 - yh, 0, keepdims=False).astype(BF16)
        away = swap(away, "yh")

    with jax.named_scope("keys"):
        starts = [sum(CHUNKS[:i]) for i in range(len(CHUNKS))]

    def outer_step(away):
        own_sum = lax.dynamic_index_in_dim(line, yh, 0, keepdims=False) + away.astype(F32)
        mean_delta = own_sum / 16
        new_momentum = MOMENTUM_DECAY * outer_momentum + mean_delta
        own_start = ((yh * 4 + x) * 2 + c) * rows
        own_synced = lax.dynamic_slice_in_dim(synced_fragment, own_start, rows, 0).astype(F32)
        own_new = (own_synced - OUTER_RATE * (mean_delta + MOMENTUM_DECAY * new_momentum)).astype(BF16)
        return own_new, new_momentum

    gain = key_gain.reshape(1, HEAD)
    contract = (((0,), (0,)), ((), ()))
    count = len(CHUNKS)
    arrived = [None] * count
    with jax.named_scope("keys"):
        second = others[1]
        for step in range(min(2, count)):
            partial = chunk_keys(second, weights, starts[step], CHUNKS[step], BF16, first)
            arrived[step] = swap(partial, "yl")
        second, arrived[0] = tie(second, arrived[0])
        partial = [
            chunk_keys(second, weights, starts[step], CHUNKS[step], BF16, first) if step >= 2 else None
            for step in range(count)
        ]

    totals, came = [], []
    out = None
    for step in range(count + 2):
        if step < count:
            start, size = starts[step], CHUNKS[step]
            with jax.named_scope("keys"):
                if step == 2:
                    arrived[step], away = tie(arrived[step], away)
                back = head_back(own_keys, arrived[step], key_cotangent, gain, inv, start)
                if step >= 1:
                    back, to_next, to_prev = tie(back, to_next, to_prev)
                    came.append((up(to_next, "z"), down(to_prev, "z")))
                other_back = swap(back, "yl")
                if step + 2 < count:
                    held, back = tie(partial[step + 2], back)
                    arrived[step + 2] = swap(held, "yl")
                if step == 2:
                    own_new, new_momentum = outer_step(away)
                    held, back = tie(own_new, back)
                    far_new = swap(held, "yh")
                if step == 3:
                    other_back, far_new, *held = tie(other_back, far_new, *came[1])
                    came[1] = held
                    here = jnp.where(
                        yh == 0, jnp.stack([own_new, far_new]), jnp.stack([far_new, own_new])
                    )
                    x_prev, x_next = up(here, "x"), down(here, "x")
                    across = jnp.stack([up(x_prev[0], "x"), down(x_next[1], "x")])
            with jax.named_scope("gradient"):
                total = lax.dot_general(mine, back, contract, preferred_element_type=F32)
                tile = other_back.shape[0] // 2
                for part in range(2):
                    total = total + lax.dot_general(
                        others[part],
                        other_back[part * tile : (part + 1) * tile],
                        contract,
                        preferred_element_type=F32,
                    )
                totals.append(total.astype(BF16))

        with jax.named_scope("gradient"):
            to_next, to_prev = payload(
                totals[step] if step < count else None,
                totals[step - 2] if step >= 2 else None,
                came[step - 2] if step >= 2 else None,
            )
            if step >= count - 1:
                came.append((up(to_next, "z"), down(to_prev, "z")))

    with jax.named_scope("gradient"):
        for step in range(count):
            out = finish(
                totals[step], came[step], came[step + 2], out, starts[step], width
            )
    with jax.named_scope("fragment_gather"):
        line = [here, x_next, across, x_prev]
        mates = [swap(value, "c") for value in line]
        new_synced = place(x, c, jnp.stack(line), jnp.stack(mates))
    return (out[None], new_synced, new_momentum)


def solution(mesh):
    fine = Mesh(mesh.devices.reshape(2, 4, 2, 2, 4), AXES)
    return jax.shard_map(
        on_device,
        mesh=fine,
        in_specs=(
            P(AXES, None),
            P(),
            P(REP, FSDP, None),
            P(),
            P(AXES, None),
            P(REP, FSDP, None),
            P(FSDP, None),
            P(FSDP + REP, None),
        ),
        out_specs=(P(REP, FSDP, None), P(FSDP, None), P(FSDP + REP, None)),
        check_vma=False,
    )
```

```python
import functools

import jax
import jax.numpy as jnp
from jax import lax
from jax.experimental import pallas as pl
from jax.experimental.pallas import tpu as pltpu
from jax.sharding import Mesh, PartitionSpec as P

BLOCK = 128
HEAD = 128

NORM_EPSILON = 1e-05
SCALE_EPSILON = 1e-06
OUTER_RATE = 0.7
MOMENTUM_DECAY = 0.9

AXES = ("yh", "x", "c", "yl", "z")
REP = ("yh", "x", "c")
FSDP = ("yl", "z")
CHUNKS = (256, 256, 256, 256)

F32 = jnp.float32
BF16 = jnp.bfloat16


def shift(value, axis, size, step):
    return lax.ppermute(value, axis, [(i, (i + step) % size) for i in range(size)])


def up(value, axis):
    return shift(value, axis, 4, 1)


def down(value, axis):
    return shift(value, axis, 4, 3)


def swap(value, axis):
    return shift(value, axis, 2, 1)


def block_terms(synced, local):
    delta = synced.astype(F32) - local.astype(F32)
    top = jnp.max(jnp.abs(delta), axis=-1, keepdims=True)
    scale = (top + SCALE_EPSILON).astype(BF16).astype(F32)
    level = (delta / scale).astype(BF16).astype(F32)
    return level * scale


def terms_kernel(pick, synced_ref, local_ref, *refs):
    out_ref = refs[-1]
    for group in range(out_ref.shape[0]):
        for start in range(0, out_ref.shape[-1], BLOCK):
            at = (group, slice(None), slice(start, start + BLOCK))
            src = (0, group, 0, slice(None), slice(start, start + BLOCK))
            terms = block_terms(synced_ref[src], local_ref[src])
            if len(refs) > 1:
                terms = terms + refs[0][at].astype(F32)
            out_ref[at] = terms.astype(BF16)


def half_terms(half, core, synced, local, other=None):
    _, groups, _, rows, width = synced.shape
    block = 2
    picked = pl.BlockSpec((1, block, 1, rows, width), lambda i, p: (half, i, p[0], 0, 0))
    plain = pl.BlockSpec((block, rows, width), lambda i, p: (i, 0, 0))
    operands = (synced, local) if other is None else (synced, local, other)
    count = groups * rows * width
    return pl.pallas_call(
        terms_kernel,
        out_shape=jax.ShapeDtypeStruct((groups, rows, width), BF16),
        grid_spec=pltpu.PrefetchScalarGridSpec(
            num_scalar_prefetch=1,
            grid=(groups // block,),
            in_specs=[picked, picked] + [plain] * (len(operands) - 2),
            out_specs=plain,
        ),
        compiler_params=pltpu.CompilerParams(vmem_limit_bytes=56 << 20),
        cost_estimate=pl.CostEstimate(
            flops=12 * count, bytes_accessed=2 * count * (len(operands) + 1), transcendentals=0
        ),
        name="block_terms",
    )(core.reshape(1), *operands)


def keys_kernel(order, tokens_ref, weight_ref, *refs):
    out_ref, total = refs[-2:]
    step = pl.program_id(0)
    part = jnp.dot(tokens_ref[...], weight_ref[...], preferred_element_type=F32)

    @pl.when(step == 0)
    def _():
        total[...] = part

    @pl.when(step > 0)
    def _():
        total[...] += part

    @pl.when(step == pl.num_programs(0) - 1)
    def _():
        if len(refs) == 2:
            out_ref[...] = total[...].astype(out_ref.dtype)
        else:
            rows = refs[0].shape[0]
            out_ref[:rows] = refs[0][...]
            out_ref[rows:] = total[...].astype(BF16)


def chunk_keys(order, tokens, weights, start, size, dtype, first=None):
    rows, depth = tokens.shape
    block = depth // 4
    specs = [
        pl.BlockSpec((rows, block), lambda i, p: (0, p[i])),
        pl.BlockSpec((block, size), lambda i, p: (i, start // size)),
    ]
    operands = [tokens, weights]
    shape = jax.ShapeDtypeStruct((rows, size), dtype)
    if first is not None:
        specs.append(pl.BlockSpec((rows, size), lambda i, p: (0, start // size)))
        operands.append(first)
        shape = jax.ShapeDtypeStruct((2 * rows, size), dtype)
    return pl.pallas_call(
        keys_kernel,
        out_shape=shape,
        grid_spec=pltpu.PrefetchScalarGridSpec(
            num_scalar_prefetch=1,
            grid=(4,),
            in_specs=specs,
            out_specs=pl.BlockSpec(shape.shape, lambda i, p: (0, 0)),
            scratch_shapes=[pltpu.VMEM((rows, size), F32)],
        ),
        compiler_params=pltpu.CompilerParams(vmem_limit_bytes=20 << 20),
        cost_estimate=pl.CostEstimate(
            flops=2 * rows * depth * size,
            bytes_accessed=2 * (rows * depth + depth * size + 3 * rows * size),
            transcendentals=0,
        ),
        name="chunk_keys",
    )(order, *operands)


def back_kernel(own_ref, other_ref, cotangent_ref, gain_ref, inv_ref, out_ref):
    gain = gain_ref[...]
    token_inv = inv_ref[...]
    for start in range(0, out_ref.shape[-1], HEAD):
        at = (slice(None), slice(start, start + HEAD))
        key = (own_ref[at] + other_ref[at].astype(F32)) * token_inv
        pulled = cotangent_ref[at].astype(F32) * gain
        inv = lax.rsqrt(jnp.mean(key * key, axis=-1, keepdims=True) + NORM_EPSILON)
        along = jnp.mean(key * pulled, axis=-1, keepdims=True)
        back = inv * pulled - key * (inv * inv * inv * along)
        out_ref[at] = (back * token_inv).astype(BF16)


def head_back(own, other, cotangent, gain, inv, start):
    rows, width = other.shape
    count = rows * width
    at = pl.BlockSpec((rows, width), lambda i: (0, start // width))
    spec = pl.BlockSpec((rows, width), lambda i: (0, 0))
    return pl.pallas_call(
        back_kernel,
        out_shape=jax.ShapeDtypeStruct((rows, width), BF16),
        grid=(1,),
        in_specs=[
            at,
            spec,
            at,
            pl.BlockSpec((1, HEAD), lambda i: (0, 0)),
            pl.BlockSpec((rows, 1), lambda i: (0, 0)),
        ],
        out_specs=spec,
        compiler_params=pltpu.CompilerParams(vmem_limit_bytes=10 << 20),
        cost_estimate=pl.CostEstimate(
            flops=16 * count, bytes_accessed=10 * count, transcendentals=count // HEAD
        ),
        name="head_back",
    )(own, other, cotangent, gain, inv)


def payload_kernel(pick, *refs, fresh, relayed):
    ins, outs = refs[:-2], refs[-2:]
    cut = outs[0].shape[0] // (2 * fresh + relayed)
    for side, out_ref in enumerate(outs):
        if fresh:
            out_ref[:cut] = ins[2 * side][...]
            out_ref[cut : 2 * cut] = ins[2 * side + 1][...]
        if relayed:
            total, arrived = ins[4 * fresh + 2 * side], ins[4 * fresh + 2 * side + 1]
            out_ref[2 * cut * fresh :] = (total[...].astype(F32) + arrived[...].astype(F32)).astype(BF16)


def payload(pick, total, before, came):
    source = total if total is not None else before
    cut, width = source.shape[0] // 8, source.shape[1]
    fresh, relayed = int(total is not None), int(before is not None)
    operands, specs = [], []

    def block(value, slot):
        operands.append(value)
        specs.append(pl.BlockSpec((cut, width), lambda i, p: (p[slot], 0)))

    if fresh:
        for slot in range(4):
            block(total, slot)
    if relayed:
        for side in range(2):
            block(before, 4 + side)
            operands.append(came[side])
            specs.append(pl.BlockSpec((cut, width), lambda i, p: (0, 0)))
    shape = jax.ShapeDtypeStruct(((2 * fresh + relayed) * cut, width), BF16)
    out_spec = pl.BlockSpec(shape.shape, lambda i, p: (0, 0))
    return pl.pallas_call(
        functools.partial(payload_kernel, fresh=fresh, relayed=relayed),
        out_shape=(shape, shape),
        grid_spec=pltpu.PrefetchScalarGridSpec(
            num_scalar_prefetch=1, grid=(1,), in_specs=specs, out_specs=(out_spec, out_spec)
        ),
        compiler_params=pltpu.CompilerParams(vmem_limit_bytes=10 << 20),
        cost_estimate=pl.CostEstimate(
            flops=4 * cut * width, bytes_accessed=30 * cut * width, transcendentals=0
        ),
        name="gradient_payload",
    )(pick, *operands)


def final_kernel(place, own_ref, prev_ref, next_ref, up_ref, down_ref, *rest):
    out_ref = rest[-1]
    cut = up_ref.shape[0]
    low, high = slice(0, cut), slice(cut, 2 * cut)
    out_ref[low] = (
        own_ref[low].astype(F32) + next_ref[...].astype(F32) + up_ref[...].astype(F32)
    ).astype(BF16)
    out_ref[high] = (
        own_ref[high].astype(F32) + prev_ref[...].astype(F32) + down_ref[...].astype(F32)
    ).astype(BF16)


def finish(place, total, came, relayed, out, start, width):
    size = total.shape[1]
    depth = total.shape[0] // 4
    cut = depth // 2
    last = relayed[0].shape[0] // cut - 1
    one = pl.BlockSpec((cut, size), lambda i, p: (1, 0))
    end = pl.BlockSpec((cut, size), lambda i, p: (last, 0))
    operands = [total, *came, *relayed]
    specs = [pl.BlockSpec((depth, size), lambda i, p: (p[0], 0)), one, one, end, end]
    aliases = {}
    if out is not None:
        operands, specs = operands + [out], specs + [pl.BlockSpec(memory_space=pl.ANY)]
        aliases = {6: 0}
    return pl.pallas_call(
        final_kernel,
        out_shape=jax.ShapeDtypeStruct((depth, width), BF16),
        grid_spec=pltpu.PrefetchScalarGridSpec(
            num_scalar_prefetch=1,
            grid=(1,),
            in_specs=specs,
            out_specs=pl.BlockSpec((depth, size), lambda i, p: (0, start // size)),
        ),
        input_output_aliases=aliases,
        compiler_params=pltpu.CompilerParams(vmem_limit_bytes=10 << 20),
        cost_estimate=pl.CostEstimate(
            flops=4 * depth * size, bytes_accessed=12 * depth * size, transcendentals=0
        ),
        name="gradient_final",
    )(place, *operands)


def place_kernel(where, own_ref, other_ref, out_ref):
    for core in range(2):
        mine = where[0] == core

        @pl.when(mine)
        def _():
            out_ref[:, 0, core] = own_ref[0]

        @pl.when(jnp.logical_not(mine))
        def _():
            out_ref[:, 0, core] = other_ref[0]


def place(x, c, own, other):
    _, _, rows, width = own.shape
    source = pl.BlockSpec((1, 2, rows, width), lambda i, w: ((i + 4 - w[1]) % 4, 0, 0, 0))
    out = pl.pallas_call(
        place_kernel,
        out_shape=jax.ShapeDtypeStruct((2, 4, 2, rows, width), BF16),
        grid_spec=pltpu.PrefetchScalarGridSpec(
            num_scalar_prefetch=1,
            grid=(4,),
            in_specs=[source, source],
            out_specs=pl.BlockSpec((2, 1, 2, rows, width), lambda i, w: (0, i, 0, 0, 0)),
        ),
        compiler_params=pltpu.CompilerParams(vmem_limit_bytes=10 << 20),
        cost_estimate=pl.CostEstimate(
            flops=0, bytes_accessed=64 * rows * width, transcendentals=0
        ),
        name="place_rows",
    )(jnp.stack([c, x]).astype(jnp.int32), own, other)
    return out.reshape(16 * rows, width)


def columns_kernel(half, in_ref, gain_ref, out_ref):
    out_ref[...] = (in_ref[...].astype(F32) * gain_ref[...]).astype(BF16)


def columns(tokens, gain, half, part):
    rows, width = tokens.shape[0] // 2, tokens.shape[1] // 2
    tile = rows // 2
    steps = rows // tile
    return pl.pallas_call(
        columns_kernel,
        out_shape=jax.ShapeDtypeStruct((rows, width), tokens.dtype),
        grid_spec=pltpu.PrefetchScalarGridSpec(
            num_scalar_prefetch=1,
            grid=(rows // tile,),
            in_specs=[
                pl.BlockSpec((tile, width), lambda i, p: (part * steps + i, p[0])),
                pl.BlockSpec((1, width), lambda i, p: (0, p[0])),
            ],
            out_specs=pl.BlockSpec((tile, width), lambda i, p: (i, 0)),
        ),
        compiler_params=pltpu.CompilerParams(vmem_limit_bytes=56 << 20),
        cost_estimate=pl.CostEstimate(
            flops=0, bytes_accessed=4 * rows * width, transcendentals=0
        ),
        name="token_columns",
    )(half.reshape(1), tokens, gain)


def columns_norm_kernel(half, in_ref, gain_ref, out_ref, inv_ref):
    width = out_ref.shape[1]
    floats = in_ref[...].astype(F32)
    mean_sq = jnp.mean(floats * floats, axis=-1, keepdims=True)
    inv_ref[...] = lax.rsqrt(mean_sq + NORM_EPSILON)
    for side in range(2):

        @pl.when(half[0] == side)
        def _():
            at = (slice(None), slice(side * width, (side + 1) * width))
            out_ref[...] = (in_ref[at].astype(F32) * gain_ref[at]).astype(BF16)


def columns_norm(tokens, gain, half):
    rows, width = tokens.shape[0], tokens.shape[1] // 2
    tile = rows // 8
    return pl.pallas_call(
        columns_norm_kernel,
        out_shape=(
            jax.ShapeDtypeStruct((rows, width), tokens.dtype),
            jax.ShapeDtypeStruct((rows, 1), F32),
        ),
        grid_spec=pltpu.PrefetchScalarGridSpec(
            num_scalar_prefetch=1,
            grid=(rows // tile,),
            in_specs=[
                pl.BlockSpec((tile, 2 * width), lambda i, p: (i, 0)),
                pl.BlockSpec((1, 2 * width), lambda i, p: (0, 0)),
            ],
            out_specs=(
                pl.BlockSpec((tile, width), lambda i, p: (i, 0)),
                pl.BlockSpec((tile, 1), lambda i, p: (i, 0)),
            ),
        ),
        compiler_params=pltpu.CompilerParams(vmem_limit_bytes=56 << 20),
        cost_estimate=pl.CostEstimate(
            flops=4 * rows * width, bytes_accessed=6 * rows * width, transcendentals=rows
        ),
        name="token_norm",
    )(half.reshape(1), tokens, gain)


def tie(*values):
    return lax.optimization_barrier(values)


def on_device(
    tokens,
    norm_gain,
    key_weight,
    key_gain,
    key_cotangent,
    local_fragment,
    synced_fragment,
    outer_momentum,
):
    c, x, yh = lax.axis_index("c"), lax.axis_index("x"), lax.axis_index("yh")
    y, z = lax.axis_index("yl"), lax.axis_index("z")
    depth, width = key_weight.shape[1:]
    cut = depth // 2

    token_gain = norm_gain.reshape(1, -1)
    with jax.named_scope("token_exchange"):
        sent = [columns(tokens, token_gain, 1 - y, part) for part in range(2)]
        sent[0], local_fragment = tie(sent[0], local_fragment)
        first = swap(sent[0], "yl")
        sent[1], first = tie(sent[1], first)
        others = (first, swap(sent[1], "yl"))

    with jax.named_scope("weight_gather"):
        weight = key_weight[0]
        cut = weight.shape[0] // 2
        prev, following = up(weight, "z"), down(weight, "z")
        far = [up(prev[:cut], "z"), down(following[cut:], "z")]
        weights = jnp.concatenate([weight, prev, following] + far, axis=0)
        order = jnp.stack([z, (z + 3) % 4, (z + 1) % 4, (z + 2) % 4]).astype(jnp.int32)

    with jax.named_scope("token_norm"):
        mine, inv = columns_norm(tokens, token_gain, y)

    rows = outer_momentum.shape[0]
    frag = outer_momentum.shape[1]
    with jax.named_scope("fragment_sum"):
        groups = [v.reshape(2, 4, 2, rows, frag) for v in (synced_fragment, local_fragment[0])]
        parts = [half_terms(h, 1 - c, *groups) for h in range(2)]
        pair = [half_terms(h, c, *groups, swap(parts[h], "c")) for h in range(2)]

        def toward(h, step):
            return lax.dynamic_index_in_dim(pair[h], (x + step) % 4, 0, keepdims=False)

        from_prev = up(jnp.stack([toward(0, 2), toward(1, 1)]), "x")
        from_next = down(jnp.stack([toward(0, 3), toward(1, 2)]), "x")

    with jax.named_scope("keys"):
        first = chunk_keys(order, others[0], weights, 0, width, BF16)
        own_keys = chunk_keys(order, mine, weights, 0, width, F32)
    from_prev, from_next, weights, first, own_keys, others = tie(
        from_prev, from_next, weights, first, own_keys, others
    )

    with jax.named_scope("fragment_sum"):
        relay_up = up((toward(0, 1).astype(F32) + from_prev[0].astype(F32)).astype(BF16), "x")
        relay_down = down((toward(1, 3).astype(F32) + from_next[1].astype(F32)).astype(BF16), "x")
        line = jnp.stack(
            [
                toward(0, 0).astype(F32) + from_next[0].astype(F32) + relay_up.astype(F32),
                toward(1, 0).astype(F32) + from_prev[1].astype(F32) + relay_down.astype(F32),
            ]
        )
        away = lax.dynamic_index_in_dim(line, 1 - yh, 0, keepdims=False).astype(BF16)
        away = swap(away, "yh")

    with jax.named_scope("keys"):
        starts = [sum(CHUNKS[:i]) for i in range(len(CHUNKS))]

    def outer_step(away):
        own_sum = lax.dynamic_index_in_dim(line, yh, 0, keepdims=False) + away.astype(F32)
        mean_delta = own_sum / 16
        new_momentum = MOMENTUM_DECAY * outer_momentum + mean_delta
        own_start = ((yh * 4 + x) * 2 + c) * rows
        own_synced = lax.dynamic_slice_in_dim(synced_fragment, own_start, rows, 0).astype(F32)
        own_new = (own_synced - OUTER_RATE * (mean_delta + MOMENTUM_DECAY * new_momentum)).astype(BF16)
        return own_new, new_momentum

    gain = key_gain.reshape(1, HEAD)
    contract = (((0,), (0,)), ((), ()))
    count = len(CHUNKS)
    arrived = [None] * count
    with jax.named_scope("keys"):
        second = others[1]
        for step in range(min(2, count)):
            partial = chunk_keys(order, second, weights, starts[step], CHUNKS[step], BF16, first)
            arrived[step] = swap(partial, "yl")
        second, arrived[0] = tie(second, arrived[0])
        partial = [
            chunk_keys(order, second, weights, starts[step], CHUNKS[step], BF16, first) if step >= 2 else None
            for step in range(count)
        ]

    pick = [(z + away) % 4 * 2 + h for away, h in ((2, 0), (1, 1), (2, 1), (3, 0), (1, 0), (3, 1))]
    pick = jnp.stack(pick).astype(jnp.int32)
    totals, came = [], []
    out = None
    for step in range(count + 2):
        if step < count:
            start, size = starts[step], CHUNKS[step]
            with jax.named_scope("keys"):
                if step == 2:
                    arrived[step], away = tie(arrived[step], away)
                back = head_back(own_keys, arrived[step], key_cotangent, gain, inv, start)
                if step >= 1:
                    back, to_next, to_prev = tie(back, to_next, to_prev)
                    came.append((up(to_next, "z"), down(to_prev, "z")))
                other_back = swap(back, "yl")
                if step + 2 < count:
                    held, back = tie(partial[step + 2], back)
                    arrived[step + 2] = swap(held, "yl")
                if step == 2:
                    own_new, new_momentum = outer_step(away)
                    held, back = tie(own_new, back)
                    far_new = swap(held, "yh")
                if step == 3:
                    other_back, far_new, *held = tie(other_back, far_new, *came[1])
                    came[1] = held
                    here = jnp.where(
                        yh == 0, jnp.stack([own_new, far_new]), jnp.stack([far_new, own_new])
                    )
                    x_prev, x_next = up(here, "x"), down(here, "x")
                    across = jnp.stack([up(x_prev[0], "x"), down(x_next[1], "x")])
                    line = jnp.stack([here, x_next, across, x_prev])
            with jax.named_scope("gradient"):
                total = lax.dot_general(mine, back, contract, preferred_element_type=F32)
                tile = other_back.shape[0] // 2
                for part in range(2):
                    total = total + lax.dot_general(
                        others[part],
                        other_back[part * tile : (part + 1) * tile],
                        contract,
                        preferred_element_type=F32,
                    )
                totals.append(total.astype(BF16))

        with jax.named_scope("gradient"):
            to_next, to_prev = payload(
                pick,
                totals[step] if step < count else None,
                totals[step - 2] if step >= 2 else None,
                came[step - 2] if step >= 2 else None,
            )
            if step >= count - 1:
                came.append((up(to_next, "z"), down(to_prev, "z")))

    with jax.named_scope("gradient"):
        for step in range(count):
            if step == count - 1:
                line, out, *held = tie(line, out, *came[step + 2])
                came[step + 2] = held
            out = finish(
                z.reshape(1), totals[step], came[step], came[step + 2], out, starts[step], width
            )
    with jax.named_scope("fragment_gather"):
        new_synced = place(x, c, line, swap(line, "c"))
    return (out[None], new_synced, new_momentum)


def solution(mesh):
    fine = Mesh(mesh.devices.reshape(2, 4, 2, 2, 4), AXES)
    return jax.shard_map(
        on_device,
        mesh=fine,
        in_specs=(
            P(AXES, None),
            P(),
            P(REP, FSDP, None),
            P(),
            P(AXES, None),
            P(REP, FSDP, None),
            P(FSDP, None),
            P(FSDP + REP, None),
        ),
        out_specs=(P(REP, FSDP, None), P(FSDP, None), P(FSDP + REP, None)),
        check_vma=False,
    )
```
